32 devices in a mesh: slab: 8 (over y, x, core), band: 4 (over z).
Axes of the slice: x: 2, y: 2, z: 4, core: 2. Of those that a mesh axis runs over, the one named last changes fastest.
Arguments:
- orbitals: float32 [16, 32, 128, 512], P('slab', None, None, 'band'), may hold values from -6 to 6
- potential: float32 [16, 32, 128], P('slab'), may hold values from -1.5 to 1.5
- projector: float32 [4096, 4, 128], P('slab'), may hold values from -0.1875 to 0.1875
- strength: float32 [512, 4], P('slab'), may hold values from 2 to 20
- entry_slot: int32 [4096], P('slab'), may hold values from 0 to 191
- entry_block: int32 [4096], P('slab'), may hold values from 0 to 63
- entry_count: int32 [8], P('slab'), may hold values from 64 to 512, as said below
Outputs:
- applied: float32 [16, 32, 128, 512], P('slab', None, None, 'band')
- correlation: float32 [512, 512], P(None, 'band')
- subspace: float32 [512, 512], P(None, 'band')
The draws below stay inside these ranges and needn't reach their ends.
Inputs may be any that keep to these rules, and one draw needn't show every extreme that they name: `entry_count`: entries of a slab's list beyond its count are not part of the problem; at least one slab's list is full.
All inputs are finite; a program needn't handle non-finite values.
Results may differ from the reference program's by a relative error of at most 0.0003.
Values sent between devices are 32-bit elements; how exact they have to be, the bound alone decides.
A program may use at most 192 MiB of HBM per device.

```python
import math
import jax
import jax.numpy as jnp
from jax import lax

ORB = 512
CZ = 2
NY = 32
NX = 128
PROJ = 4
ATOM_DEV = 64
ENT_DEV = 512
SLABS = 8
NZ = 16
ATOMS = 512
ENTRIES = 4096


def draw_entry_count(key, part):
    key = jax.random.fold_in(key, 11)
    sub_one, sub_two = jax.random.split(key)
    first_slab = jax.random.randint(sub_one, (), 0, SLABS)
    slab_index = jnp.arange(SLABS, dtype=jnp.int32)
    inside = (slab_index - first_slab) % SLABS < max(SLABS // 3, 1)
    light_load = jax.random.randint(sub_two, (SLABS,), ENT_DEV // 8, ENT_DEV // 2 + 1)
    return jnp.where(inside, ENT_DEV, light_load).astype(jnp.int32)


def plant(values, stream_key, least, top_value):
    longest = values.shape.index(max(values.shape))
    spots = []
    for shift in (0, 1):
        where = [jax.random.randint(jax.random.fold_in(stream_key, axis), (), 0, length) for axis, length in enumerate(values.shape)]
        where[longest] = (where[longest] + shift) % values.shape[longest]
        spots.append(tuple(where))
    return values.at[spots[0]].set(least).at[spots[1]].set(top_value)


def levels(stream_key, shape, shards, smallest, high):
    factor_of = 1.0
    for position, parts in shards:
        heights = jax.random.uniform(jax.random.fold_in(jax.random.fold_in(stream_key, 6), position), (parts,), jnp.float32, smallest / len(shards), high / len(shards))
        factor_of = factor_of * jnp.repeat(jnp.exp(heights), shape[position] // parts).reshape((-1,) + (1,) * (len(shape) - 1 - position))
    return factor_of


def noise(own_key, dims, scale, bound, shards=(), kind=jnp.bfloat16):
    array = jax.random.normal(own_key, dims, jnp.float32) * scale
    if len(shards) > 0:
        array = levels(own_key, dims, shards, -0.22, 0.18) * array
    return jnp.clip(array, min=-bound, max=bound).astype(kind)


def setup_inputs(seed: int = 0) -> dict:
    seeds = jax.random.split(jax.random.key(seed), 8)
    return {
        "orbitals": noise(seeds[0], (NZ, NY, NX, ORB), 1.0, 6.0, ((0, 8), (3, 4)), jnp.float32),
        "potential": jnp.clip(jax.random.uniform(seeds[1], (NZ, NY, NX), jnp.float32, -1.5, 1.5) * levels(seeds[1], (NZ, NY, NX), ((0, 8),), -0.4, 0.0), -1.5, 1.5),
        "projector": noise(seeds[2], (ENTRIES, PROJ, NX), (NX * 8) ** -0.5, 0.1875, ((0, 8),), jnp.float32),
        "strength": jnp.clip(jnp.exp(math.log(20.0) - 2.3025851 * jax.random.uniform(seeds[3], (ATOMS, PROJ), jnp.float32) ** levels(seeds[3], (ATOMS, PROJ), ((0, 8),), -0.2, 0.2)), 2.0, 20.0),
        "entry_slot": plant(jax.random.randint(seeds[4], (ENTRIES,), 0, 3 * ATOM_DEV), jax.random.fold_in(seeds[4], 1), 0, (3 * ATOM_DEV) - 1).astype(jnp.int32),
        "entry_block": plant(jax.random.randint(seeds[5], (ENTRIES,), 0, CZ * NY), jax.random.fold_in(seeds[5], 1), 0, (CZ * NY) - 1).astype(jnp.int32),
        "entry_count": draw_entry_count(jax.random.fold_in(seeds[7], 71), 0),
    }


centre_coef = -2.5
near_coef = 4.0 / 3.0
far_coef = -1.0 / 12.0
highest = lax.Precision.HIGHEST


def laplace(field_in):
    summed = 3.0 * centre_coef * field_in
    for axis_num in range(3):
        summed = summed + near_coef * (jnp.roll(field_in, 1, axis_num) + jnp.roll(field_in, -1, axis_num))
        summed = summed + far_coef * (jnp.roll(field_in, 2, axis_num) + jnp.roll(field_in, -2, axis_num))
    return summed


def live_weights(slot_ids, count_now, slot_width):
    positions = jnp.arange(slot_ids.shape[0], dtype=jnp.int32)
    sections = lax.broadcasted_iota(jnp.int32, (slot_width, slot_ids.shape[0]), 0)
    return ((slot_ids[None, :] == sections) & (positions < count_now)[None, :]).astype(jnp.float32)


def reference(orbitals, potential, projector, strength, entry_slot, entry_block, entry_count):
    grid_rows = orbitals.reshape(NZ * NY, NX, ORB)
    slot_width = 3 * ATOM_DEV
    slab_list = jnp.arange(SLABS, dtype=jnp.int32)

    def entry_data(slab_num):
        first_entry = slab_num * ENT_DEV
        block_ids = lax.dynamic_slice_in_dim(entry_block, first_entry, ENT_DEV, 0)
        slot_ids = lax.dynamic_slice_in_dim(entry_slot, first_entry, ENT_DEV, 0)
        values = lax.dynamic_slice_in_dim(projector, first_entry, ENT_DEV, 0)
        onehot = live_weights(slot_ids, entry_count[slab_num], slot_width)
        return block_ids, values, onehot

    def slab_partial(slab_num):
        block_ids, values, onehot = entry_data(slab_num)
        slab_rows = lax.dynamic_slice_in_dim(grid_rows, slab_num * CZ * NY, CZ * NY, 0)
        picked = slab_rows[block_ids]
        products = jnp.einsum('epc,eco->epo', values, picked, precision=highest)
        return jnp.einsum('se,epo->spo', onehot, products, precision=highest)

    partials = lax.map(slab_partial, slab_list).reshape(SLABS, 3, ATOM_DEV, PROJ, ORB)
    coefficient = partials[:, 1] + jnp.roll(partials[:, 2], 1, 0) + jnp.roll(partials[:, 0], -1, 0)
    scaled = strength.reshape(SLABS, ATOM_DEV, PROJ)[..., None] * coefficient
    sections = jnp.concatenate([jnp.roll(scaled, 1, 0), scaled, jnp.roll(scaled, -1, 0)], axis=1)

    def slab_apply(slab_num):
        block_ids, values, onehot = entry_data(slab_num)
        coef_entry = jnp.einsum('se,spo->epo', onehot, sections[slab_num], precision=highest)
        contrib = jnp.einsum('epc,epo->eco', values, coef_entry, precision=highest)
        return jnp.zeros((CZ * NY, NX, ORB), jnp.float32).at[block_ids].add(contrib)

    sphere_part = lax.map(slab_apply, slab_list).reshape(NZ, NY, NX, ORB)
    applied = -0.5 * laplace(orbitals) + potential[..., None] * orbitals + sphere_part
    volume = 1.0 / (NZ * NY * NX)
    contract = (((0,), (0,)), ((), ()))
    flat_orb = orbitals.reshape(-1, ORB)
    flat_img = applied.reshape(-1, ORB)
    correlation = lax.dot_general(flat_orb, flat_orb, contract, precision=highest, preferred_element_type=jnp.float32) * volume
    subspace = lax.dot_general(flat_orb, flat_img, contract, precision=highest, preferred_element_type=jnp.float32) * volume
    return applied, correlation, subspace
```

```python
import functools

import jax
import jax.numpy as jnp
from jax import lax
from jax.experimental import pallas as pl
from jax.experimental.pallas import tpu as pltpu
from jax.sharding import PartitionSpec as P

centre_coef = -2.5
near_coef = 4.0 / 3.0
far_coef = -1.0 / 12.0
highest = lax.Precision.HIGHEST
MIB = 1 << 20

first_round = ((0, 3), (3, 1), (1, 2), (2, 0))
second_round = ((0, 1), (3, 2))


def project_kernel(slots, slot_ref, block_ref, count_ref, projector_ref, x_ref, w_ref, part_ref):
    rows = x_ref.shape[0]
    channels = projector_ref.shape[1]

    @pl.loop(0, rows)
    def _(row):
        w_ref[row] = jnp.zeros(w_ref.shape[1:], jnp.float32)

    @pl.loop(0, count_ref[0])
    def _(entry):
        slot = slot_ref[entry]
        row = block_ref[entry]
        for channel in range(channels):
            place = pl.ds(channel * slots + slot, 1)
            w_ref[row, place, :] = (
                w_ref[row, place, :] + projector_ref[entry, pl.ds(channel, 1), :]
            )

    part_ref[...] = jnp.zeros_like(part_ref)

    @pl.loop(0, rows)
    def _(row):
        part_ref[...] += jnp.dot(
            w_ref[row], x_ref[row], precision=highest, preferred_element_type=jnp.float32
        )


def project(entry_slot, entry_block, entry_count, projector, grid_rows, slots):
    rows, cells, cols = grid_rows.shape
    channels = projector.shape[1]
    smem = pl.BlockSpec(memory_space=pltpu.SMEM)
    vmem = pl.BlockSpec(memory_space=pltpu.VMEM)
    return pl.pallas_call(
        functools.partial(project_kernel, slots),
        out_shape=(
            jax.ShapeDtypeStruct((rows, channels * slots, cells), jnp.float32),
            jax.ShapeDtypeStruct((channels * slots, cols), jnp.float32),
        ),
        in_specs=[smem, smem, smem, vmem, vmem],
        out_specs=(vmem, vmem),
        compiler_params=pltpu.CompilerParams(vmem_limit_bytes=48 * MIB),
        cost_estimate=pl.CostEstimate(
            flops=12 * rows * channels * slots * cells * cols,
            bytes_accessed=4 * rows * channels * slots * cells,
            transcendentals=0,
        ),
        name="project",
    )(entry_slot, entry_block, entry_count, projector, grid_rows)


def apply_kernel(x_ref, before_ref, after_ref, potential_ref, scaled_ref, w_ref, out_ref):
    planes, height, cells, cols = x_ref.shape
    y = pl.program_id(0)

    def plane(z, at):
        if z < 0:
            return before_ref[planes + z, at]
        if z >= planes:
            return after_ref[z - planes, at]
        return x_ref[z, at]

    for z in range(planes):
        centre = x_ref[z, y]
        near = plane(z - 1, y) + plane(z + 1, y)
        far = plane(z - 2, y) + plane(z + 2, y)
        near += x_ref[z, lax.rem(y + 1, height)] + x_ref[z, lax.rem(y + height - 1, height)]
        far += x_ref[z, lax.rem(y + 2, height)] + x_ref[z, lax.rem(y + height - 2, height)]
        near += pltpu.roll(centre, 1, 0) + pltpu.roll(centre, cells - 1, 0)
        far += pltpu.roll(centre, 2, 0) + pltpu.roll(centre, cells - 2, 0)
        level = jnp.broadcast_to(potential_ref[z, pl.ds(y, 1), :], (cols, cells)).T
        sphere = lax.dot_general(
            w_ref[z, 0],
            scaled_ref[...],
            (((0,), (0,)), ((), ())),
            precision=highest,
            preferred_element_type=jnp.float32,
        )
        out_ref[z, 0] = (
            (level - 1.5 * centre_coef) * centre
            - 0.5 * near_coef * near
            - 0.5 * far_coef * far
            + sphere
        )


def apply(orbitals, before, after, potential, scaled, weights):
    planes, height, cells, cols = orbitals.shape
    depth = weights.shape[1]
    vmem = pl.BlockSpec(memory_space=pltpu.VMEM)
    return pl.pallas_call(
        apply_kernel,
        grid=(height,),
        out_shape=jax.ShapeDtypeStruct(orbitals.shape, jnp.float32),
        in_specs=[vmem] * 5 + [pl.BlockSpec((planes, 1, depth, cells), lambda y: (0, y, 0, 0))],
        out_specs=pl.BlockSpec((planes, 1, cells, cols), lambda y: (0, y, 0, 0)),
        compiler_params=pltpu.CompilerParams(vmem_limit_bytes=48 * MIB),
        cost_estimate=pl.CostEstimate(
            flops=12 * planes * height * depth * cells * cols,
            bytes_accessed=4 * planes * height * depth * cells,
            transcendentals=0,
        ),
        name="apply",
    )(orbitals, before, after, potential, scaled, weights.reshape(planes, height, depth, cells))


def products(left, orbitals, applied):
    cols = orbitals.shape[-1]
    left = left.reshape(-1, cols)
    contract = (((0,), (0,)), ((), ()))
    return jnp.stack(
        [
            lax.dot_general(
                left,
                right.reshape(-1, cols),
                contract,
                precision=lax.Precision.HIGH,
                preferred_element_type=jnp.float32,
            )
            for right in (orbitals, applied)
        ]
    )


def local(orbitals, potential, projector, strength, entry_slot, entry_block, entry_count):
    planes, height, cells, cols = orbitals.shape
    atom_slots, channels = strength.shape
    slots = 3 * atom_slots
    slabs = lax.axis_size("slab")
    up = [(i, (i + 1) % slabs) for i in range(slabs)]
    down = [(j, i) for i, j in up]
    band = lax.axis_index("band")

    before = lax.ppermute(orbitals, "slab", up)
    after = lax.ppermute(orbitals, "slab", down)
    met_second = lax.ppermute(orbitals, "band", second_round)
    met_first = lax.ppermute(orbitals, "band", first_round)

    weights, partial_value = project(
        entry_slot,
        entry_block,
        entry_count,
        projector,
        orbitals.reshape(planes * height, cells, cols),
        slots,
    )
    partial_value = partial_value.reshape(channels, 3, atom_slots, cols)
    from_left = lax.ppermute(partial_value[:, 2], "slab", up)
    from_right = lax.ppermute(partial_value[:, 0], "slab", down)
    coefficient = partial_value[:, 1] + from_left + from_right
    scaled = strength.T[:, :, None] * coefficient
    beside_all = jnp.stack(
        [lax.ppermute(scaled, "slab", up), scaled, lax.ppermute(scaled, "slab", down)], axis=1
    ).reshape(channels * slots, cols)

    applied = apply(orbitals, before, after, potential, beside_all, weights)

    volume = 1.0 / (slabs * planes * height * cells)
    early = jnp.stack(
        [products(orbitals, orbitals, applied), products(met_second, orbitals, applied)]
    )
    own, second = lax.psum(early * volume, "slab")
    first = lax.psum(products(met_first, orbitals, applied) * volume, "slab")

    def mirror(blocks, pairs):
        return lax.ppermute(
            jnp.swapaxes(blocks, 1, 2), "band", [(there, here) for here, there in pairs]
        )

    second = second + mirror(second, second_round)
    mirrored = mirror(first, first_round)
    found = jnp.stack([own, second, first, mirrored])
    kinds = [[0] * 4 for _ in range(4)]
    for here, there in second_round:
        kinds[here][there] = kinds[there][here] = 1
    for here, there in first_round:
        kinds[there][here] = 2
        kinds[here][there] = 3
    order = jnp.array(kinds, jnp.int32)[band]
    rows = jnp.concatenate(
        [lax.dynamic_index_in_dim(found, order[r], 0, keepdims=False) for r in range(4)], axis=1
    )
    return applied, rows[0], rows[1]


def solution(mesh):
    in_specs = (
        P("slab", None, None, "band"),
        P("slab", None, None),
        P("slab", None, None),
        P("slab", None),
        P("slab"),
        P("slab"),
        P("slab"),
    )
    out_specs = (P("slab", None, None, "band"), P(None, "band"), P(None, "band"))
    return jax.shard_map(local, mesh=mesh, in_specs=in_specs, out_specs=out_specs, check_vma=False)
```

```python
import functools

import jax
import jax.numpy as jnp
from jax import lax
from jax.experimental import pallas as pl
from jax.experimental.pallas import tpu as pltpu
from jax.sharding import PartitionSpec as P

centre_coef = -2.5
near_coef = 4.0 / 3.0
far_coef = -1.0 / 12.0
highest = lax.Precision.HIGHEST
MIB = 1 << 20

groups = 4
next_round = tuple((i, (i + 1) % groups) for i in range(groups))
across_round = ((0, 2), (3, 1))


def project_kernel(slots, slot_ref, block_ref, count_ref, projector_ref, x_ref, w_ref, part_ref):
    rows = x_ref.shape[0]
    channels = projector_ref.shape[1]

    @pl.loop(0, rows)
    def _(row):
        w_ref[row] = jnp.zeros(w_ref.shape[1:], jnp.float32)

    @pl.loop(0, count_ref[0])
    def _(entry):
        slot = slot_ref[entry]
        row = block_ref[entry]
        for channel in range(channels):
            place = pl.ds(channel * slots + slot, 1)
            w_ref[row, place, :] = (
                w_ref[row, place, :] + projector_ref[entry, pl.ds(channel, 1), :]
            )

    part_ref[...] = jnp.zeros_like(part_ref)

    @pl.loop(0, rows)
    def _(row):
        part_ref[...] += jnp.dot(
            w_ref[row], x_ref[row], precision=highest, preferred_element_type=jnp.float32
        )


def project(entry_slot, entry_block, entry_count, projector, grid_rows, slots):
    rows, cells, cols = grid_rows.shape
    channels = projector.shape[1]
    smem = pl.BlockSpec(memory_space=pltpu.SMEM)
    vmem = pl.BlockSpec(memory_space=pltpu.VMEM)
    return pl.pallas_call(
        functools.partial(project_kernel, slots),
        out_shape=(
            jax.ShapeDtypeStruct((rows, channels * slots, cells), jnp.float32),
            jax.ShapeDtypeStruct((channels * slots, cols), jnp.float32),
        ),
        in_specs=[smem, smem, smem, vmem, vmem],
        out_specs=(vmem, vmem),
        compiler_params=pltpu.CompilerParams(vmem_limit_bytes=48 * MIB),
        cost_estimate=pl.CostEstimate(
            flops=12 * rows * channels * slots * cells * cols,
            bytes_accessed=4 * rows * channels * slots * cells,
            transcendentals=0,
        ),
        name="project",
    )(entry_slot, entry_block, entry_count, projector, grid_rows)


def apply_kernel(x_ref, before_ref, after_ref, potential_ref, scaled_ref, w_ref, out_ref):
    planes, height, cells, cols = x_ref.shape
    y = pl.program_id(0)

    def plane(z, at):
        if z < 0:
            return before_ref[planes + z, at]
        if z >= planes:
            return after_ref[z - planes, at]
        return x_ref[z, at]

    for z in range(planes):
        centre = x_ref[z, y]
        near = plane(z - 1, y) + plane(z + 1, y)
        far = plane(z - 2, y) + plane(z + 2, y)
        near += x_ref[z, lax.rem(y + 1, height)] + x_ref[z, lax.rem(y + height - 1, height)]
        far += x_ref[z, lax.rem(y + 2, height)] + x_ref[z, lax.rem(y + height - 2, height)]
        near += pltpu.roll(centre, 1, 0) + pltpu.roll(centre, cells - 1, 0)
        far += pltpu.roll(centre, 2, 0) + pltpu.roll(centre, cells - 2, 0)
        level = jnp.broadcast_to(potential_ref[z, pl.ds(y, 1), :], (cols, cells)).T
        sphere = lax.dot_general(
            w_ref[z, 0],
            scaled_ref[...],
            (((0,), (0,)), ((), ())),
            precision=highest,
            preferred_element_type=jnp.float32,
        )
        out_ref[z, 0] = (
            (level - 1.5 * centre_coef) * centre
            - 0.5 * near_coef * near
            - 0.5 * far_coef * far
            + sphere
        )


def apply(orbitals, before, after, potential, scaled, weights):
    planes, height, cells, cols = orbitals.shape
    depth = weights.shape[1]
    vmem = pl.BlockSpec(memory_space=pltpu.VMEM)
    return pl.pallas_call(
        apply_kernel,
        grid=(height,),
        out_shape=jax.ShapeDtypeStruct(orbitals.shape, jnp.float32),
        in_specs=[vmem] * 5 + [pl.BlockSpec((planes, 1, depth, cells), lambda y: (0, y, 0, 0))],
        out_specs=pl.BlockSpec((planes, 1, cells, cols), lambda y: (0, y, 0, 0)),
        compiler_params=pltpu.CompilerParams(vmem_limit_bytes=48 * MIB),
        cost_estimate=pl.CostEstimate(
            flops=12 * planes * height * depth * cells * cols,
            bytes_accessed=4 * planes * height * depth * cells,
            transcendentals=0,
        ),
        name="apply",
    )(orbitals, before, after, potential, scaled, weights.reshape(planes, height, depth, cells))


def gram_kernel(count, *refs):
    *left_refs, x_ref, applied_ref, out_ref = refs
    bf16 = jnp.bfloat16

    def halves(values):
        high = values.astype(bf16)
        return high, (values - high.astype(jnp.float32)).astype(bf16)

    def times(left, right):
        return lax.dot_general(
            left, right, (((0,), (0,)), ((), ())), preferred_element_type=jnp.float32
        )

    @pl.when(pl.program_id(0) == 0)
    def _():
        out_ref[...] = jnp.zeros_like(out_ref)

    left_high, left_low = halves(jnp.concatenate([ref[...] for ref in left_refs], axis=1))
    right_high, right_low = halves(jnp.concatenate([x_ref[...], applied_ref[...]], axis=1))
    out_ref[...] += (
        times(left_high, right_high) + times(left_high, right_low) + times(left_low, right_high)
    )


def gram(lefts, orbitals, applied):
    cols = orbitals.shape[-1]
    cells = orbitals.size // cols
    step = min(1024, cells)
    arrays = [x.reshape(cells, cols) for x in (*lefts, orbitals, applied)]
    count = len(lefts)
    out = pl.pallas_call(
        functools.partial(gram_kernel, count),
        grid=(cells // step,),
        out_shape=jax.ShapeDtypeStruct((count * cols, 2 * cols), jnp.float32),
        in_specs=[pl.BlockSpec((step, cols), lambda i: (i, 0))] * len(arrays),
        out_specs=pl.BlockSpec((count * cols, 2 * cols), lambda i: (0, 0)),
        compiler_params=pltpu.CompilerParams(vmem_limit_bytes=32 * MIB),
        cost_estimate=pl.CostEstimate(
            flops=12 * count * cells * cols * cols,
            bytes_accessed=4 * (count + 2) * cells * cols,
            transcendentals=0,
        ),
        name="gram",
    )(*arrays)
    return jnp.swapaxes(out.reshape(count, cols, 2, cols), 1, 2)


def reduce_kernel(
    slabs, part_ref, overlap_ref, operator_ref,
    landed, summed, mirrored, gathered, send_one, recv_one, send_two, recv_two, send_three, recv_three,
):
    slab = lax.axis_index("slab")
    band = lax.axis_index("band")
    here_next = lax.rem(band + 1, groups)
    here_previous = lax.rem(band + groups - 1, groups)
    here_across = lax.rem(band + 2, groups)
    cols = overlap_ref.shape[1]
    mesh_type = pl.DeviceIdType.MESH

    barrier = pltpu.get_barrier_semaphore()

    @pl.loop(1, slabs)
    def _(d):
        pl.semaphore_signal(
            barrier, inc=1, device_id=(lax.rem(slab + d, slabs), band), device_id_type=mesh_type
        )

    for other in (here_next, here_previous, here_across):
        pl.semaphore_signal(barrier, inc=1, device_id=(slab, other), device_id_type=mesh_type)
    pl.semaphore_wait(barrier, slabs - 1 + 3)

    def scatter(d):
        peer = lax.rem(slab + d, slabs)
        return pltpu.make_async_remote_copy(
            src_ref=part_ref.at[peer],
            dst_ref=landed.at[d - 1],
            send_sem=send_one.at[d - 1],
            recv_sem=recv_one.at[d - 1],
            device_id=(peer, band),
            device_id_type=mesh_type,
        )

    @pl.loop(1, slabs)
    def _(d):
        scatter(d).start()

    summed[...] = part_ref[slab]

    @pl.loop(1, slabs)
    def _(d):
        scatter(d).wait()
        summed[...] += landed[d - 1]

    exchanges = [
        pltpu.make_async_remote_copy(
            src_ref=summed.at[block],
            dst_ref=mirrored.at[place],
            send_sem=send_two.at[place],
            recv_sem=recv_two.at[place],
            device_id=(slab, other),
            device_id_type=mesh_type,
        )
        for place, (block, other) in enumerate(((1, here_across), (2, here_previous)))
    ]
    for exchange in exchanges:
        exchange.start()
    for exchange in exchanges:
        exchange.wait()

    gave = (band == across_round[0][0]) | (band == across_round[1][0])
    gathered[slab, 0] = summed[0]
    gathered[slab, 1] = jnp.where(gave, mirrored[0], summed[1])
    gathered[slab, 2] = summed[2]
    gathered[slab, 3] = mirrored[1]

    def spread(d):
        return pltpu.make_async_remote_copy(
            src_ref=gathered.at[slab],
            dst_ref=gathered.at[slab],
            send_sem=send_three.at[d - 1],
            recv_sem=recv_three.at[d - 1],
            device_id=(lax.rem(slab + d, slabs), band),
            device_id_type=mesh_type,
        )

    @pl.loop(1, slabs)
    def _(d):
        spread(d).start()

    @pl.loop(1, slabs)
    def _(d):
        spread(d).wait()

    for block, other in enumerate((band, here_across, here_previous, here_next)):
        values = gathered[:, block].reshape(2, cols, cols)
        rows = pl.ds(pl.multiple_of(other * cols, cols), cols)
        for ref, value in ((overlap_ref, values[0]), (operator_ref, values[1])):
            if block == 1:
                value = jnp.where(gave, value.T, value)
            if block == 3:
                value = value.T
            ref[rows, :] = value


def reduce(parts, slabs):
    blocks, _, cols, _ = parts.shape
    rows = 2 * cols // slabs
    parts = jnp.swapaxes(parts.reshape(blocks, slabs, rows, cols), 0, 1)
    vmem = pl.BlockSpec(memory_space=pltpu.VMEM)
    return pl.pallas_call(
        functools.partial(reduce_kernel, slabs),
        out_shape=(jax.ShapeDtypeStruct((groups * cols, cols), jnp.float32),) * 2,
        in_specs=[vmem],
        out_specs=(vmem, vmem),
        scratch_shapes=[
            pltpu.VMEM((slabs - 1, blocks, rows, cols), jnp.float32),
            pltpu.VMEM((blocks, rows, cols), jnp.float32),
            pltpu.VMEM((2, rows, cols), jnp.float32),
            pltpu.VMEM((slabs, groups, rows, cols), jnp.float32),
            pltpu.SemaphoreType.DMA((slabs - 1,)),
            pltpu.SemaphoreType.DMA((slabs - 1,)),
            pltpu.SemaphoreType.DMA((2,)),
            pltpu.SemaphoreType.DMA((2,)),
            pltpu.SemaphoreType.DMA((slabs - 1,)),
            pltpu.SemaphoreType.DMA((slabs - 1,)),
        ],
        compiler_params=pltpu.CompilerParams(
            collective_id=0, has_side_effects=True, vmem_limit_bytes=32 * MIB
        ),
        name="reduce",
    )(parts)


def local(orbitals, potential, projector, strength, entry_slot, entry_block, entry_count):
    planes, height, cells, cols = orbitals.shape
    atom_slots, channels = strength.shape
    slots = 3 * atom_slots
    slabs = lax.axis_size("slab")
    up = [(i, (i + 1) % slabs) for i in range(slabs)]
    down = [(j, i) for i, j in up]

    before = lax.ppermute(orbitals, "slab", up)
    after = lax.ppermute(orbitals, "slab", down)
    met_across = lax.ppermute(orbitals, "band", across_round)
    met_next = lax.ppermute(orbitals, "band", next_round)

    weights, partial_value = project(
        entry_slot,
        entry_block,
        entry_count,
        projector,
        orbitals.reshape(planes * height, cells, cols),
        slots,
    )
    partial_value = partial_value.reshape(channels, 3, atom_slots, cols)
    from_left = lax.ppermute(partial_value[:, 2], "slab", up)
    from_right = lax.ppermute(partial_value[:, 0], "slab", down)
    coefficient = partial_value[:, 1] + from_left + from_right
    scaled = strength.T[:, :, None] * coefficient
    beside_all = jnp.stack(
        [lax.ppermute(scaled, "slab", up), scaled, lax.ppermute(scaled, "slab", down)], axis=1
    ).reshape(channels * slots, cols)

    applied = apply(orbitals, before, after, potential, beside_all, weights)

    volume = 1.0 / (slabs * planes * height * cells)
    early = gram((orbitals, met_across), orbitals, applied)
    late = gram((met_next,), orbitals, applied)
    correlation, subspace = reduce(jnp.concatenate([early, late]) * volume, slabs)
    return applied, correlation, subspace


def solution(mesh):
    in_specs = (
        P("slab", None, None, "band"),
        P("slab", None, None),
        P("slab", None, None),
        P("slab", None),
        P("slab"),
        P("slab"),
        P("slab"),
    )
    out_specs = (P("slab", None, None, "band"), P(None, "band"), P(None, "band"))
    return jax.shard_map(local, mesh=mesh, in_specs=in_specs, out_specs=out_specs, check_vma=False)
```

```python
import functools

import jax
import jax.numpy as jnp
from jax import lax
from jax.experimental import pallas as pl
from jax.experimental.pallas import tpu as pltpu
from jax.sharding import PartitionSpec as P

centre_coef = -2.5
near_coef = 4.0 / 3.0
far_coef = -1.0 / 12.0
highest = lax.Precision.HIGHEST
MIB = 1 << 20

groups = 4
next_round = tuple((i, (i + 1) % groups) for i in range(groups))
across_round = ((0, 2), (3, 1))


def project_kernel(slots, slot_ref, block_ref, count_ref, projector_ref, x_ref, w_ref, part_ref):
    rows = x_ref.shape[0]
    channels = projector_ref.shape[1]

    @pl.loop(0, rows)
    def _(row):
        w_ref[row] = jnp.zeros(w_ref.shape[1:], jnp.float32)

    @pl.loop(0, count_ref[0])
    def _(entry):
        slot = slot_ref[entry]
        row = block_ref[entry]
        for channel in range(channels):
            place = pl.ds(channel * slots + slot, 1)
            w_ref[row, place, :] = (
                w_ref[row, place, :] + projector_ref[entry, pl.ds(channel, 1), :]
            )

    part_ref[...] = jnp.zeros_like(part_ref)

    @pl.loop(0, rows)
    def _(row):
        part_ref[...] += jnp.dot(
            w_ref[row], x_ref[row], precision=highest, preferred_element_type=jnp.float32
        )


def project(entry_slot, entry_block, entry_count, projector, grid_rows, slots):
    rows, cells, cols = grid_rows.shape
    channels = projector.shape[1]
    smem = pl.BlockSpec(memory_space=pltpu.SMEM)
    vmem = pl.BlockSpec(memory_space=pltpu.VMEM)
    return pl.pallas_call(
        functools.partial(project_kernel, slots),
        out_shape=(
            jax.ShapeDtypeStruct((rows, channels * slots, cells), jnp.float32),
            jax.ShapeDtypeStruct((channels * slots, cols), jnp.float32),
        ),
        in_specs=[smem, smem, smem, vmem, vmem],
        out_specs=(vmem, vmem),
        compiler_params=pltpu.CompilerParams(vmem_limit_bytes=48 * MIB),
        cost_estimate=pl.CostEstimate(
            flops=12 * rows * channels * slots * cells * cols,
            bytes_accessed=4 * rows * channels * slots * cells,
            transcendentals=0,
        ),
        name="project",
    )(entry_slot, entry_block, entry_count, projector, grid_rows)


def apply_kernel(x_ref, before_ref, after_ref, potential_ref, scaled_ref, w_ref, out_ref):
    planes, height, cells, cols = x_ref.shape
    y = pl.program_id(0)

    def plane(z, at):
        if z < 0:
            return before_ref[planes + z, at]
        if z >= planes:
            return after_ref[z - planes, at]
        return x_ref[z, at]

    for z in range(planes):
        centre = x_ref[z, y]
        near = plane(z - 1, y) + plane(z + 1, y)
        far = plane(z - 2, y) + plane(z + 2, y)
        near += x_ref[z, lax.rem(y + 1, height)] + x_ref[z, lax.rem(y + height - 1, height)]
        far += x_ref[z, lax.rem(y + 2, height)] + x_ref[z, lax.rem(y + height - 2, height)]
        near += pltpu.roll(centre, 1, 0) + pltpu.roll(centre, cells - 1, 0)
        far += pltpu.roll(centre, 2, 0) + pltpu.roll(centre, cells - 2, 0)
        level = jnp.broadcast_to(potential_ref[z, pl.ds(y, 1), :], (cols, cells)).T
        sphere = lax.dot_general(
            w_ref[z, 0],
            scaled_ref[...],
            (((0,), (0,)), ((), ())),
            precision=highest,
            preferred_element_type=jnp.float32,
        )
        out_ref[z, 0] = (
            (level - 1.5 * centre_coef) * centre
            - 0.5 * near_coef * near
            - 0.5 * far_coef * far
            + sphere
        )


def apply(orbitals, before, after, potential, scaled, weights):
    planes, height, cells, cols = orbitals.shape
    depth = weights.shape[1]
    vmem = pl.BlockSpec(memory_space=pltpu.VMEM)
    return pl.pallas_call(
        apply_kernel,
        grid=(height,),
        out_shape=jax.ShapeDtypeStruct(orbitals.shape, jnp.float32),
        in_specs=[vmem] * 5 + [pl.BlockSpec((planes, 1, depth, cells), lambda y: (0, y, 0, 0))],
        out_specs=pl.BlockSpec((planes, 1, cells, cols), lambda y: (0, y, 0, 0)),
        compiler_params=pltpu.CompilerParams(vmem_limit_bytes=48 * MIB),
        cost_estimate=pl.CostEstimate(
            flops=12 * planes * height * depth * cells * cols,
            bytes_accessed=4 * planes * height * depth * cells,
            transcendentals=0,
        ),
        name="apply",
    )(orbitals, before, after, potential, scaled, weights.reshape(planes, height, depth, cells))


def gram_kernel(count, *refs):
    *left_refs, x_ref, applied_ref, out_ref = refs
    bf16 = jnp.bfloat16

    def halves(values):
        high = values.astype(bf16)
        return high, (values - high.astype(jnp.float32)).astype(bf16)

    def times(left, right):
        return lax.dot_general(
            left, right, (((0,), (0,)), ((), ())), preferred_element_type=jnp.float32
        )

    @pl.when(pl.program_id(0) == 0)
    def _():
        out_ref[...] = jnp.zeros_like(out_ref)

    left_high, left_low = halves(jnp.concatenate([ref[...] for ref in left_refs], axis=1))
    right_high, right_low = halves(jnp.concatenate([x_ref[...], applied_ref[...]], axis=1))
    out_ref[...] += (
        times(left_high, right_high) + times(left_high, right_low) + times(left_low, right_high)
    )


def gram(lefts, orbitals, applied):
    cols = orbitals.shape[-1]
    cells = orbitals.size // cols
    step = min(1024, cells)
    arrays = [x.reshape(cells, cols) for x in (*lefts, orbitals, applied)]
    count = len(lefts)
    out = pl.pallas_call(
        functools.partial(gram_kernel, count),
        grid=(cells // step,),
        out_shape=jax.ShapeDtypeStruct((count * cols, 2 * cols), jnp.float32),
        in_specs=[pl.BlockSpec((step, cols), lambda i: (i, 0))] * len(arrays),
        out_specs=pl.BlockSpec((count * cols, 2 * cols), lambda i: (0, 0)),
        compiler_params=pltpu.CompilerParams(vmem_limit_bytes=60 * MIB),
        cost_estimate=pl.CostEstimate(
            flops=12 * count * cells * cols * cols,
            bytes_accessed=4 * (count + 2) * cells * cols,
            transcendentals=0,
        ),
        name="gram",
    )(*arrays)
    return jnp.swapaxes(out.reshape(count, cols, 2, cols), 1, 2)


mesh_type = pl.DeviceIdType.MESH


def greet(slabs, others):
    slab = lax.axis_index("slab")
    band = lax.axis_index("band")
    barrier = pltpu.get_barrier_semaphore()

    @pl.loop(1, slabs)
    def _(d):
        pl.semaphore_signal(
            barrier, inc=1, device_id=(lax.rem(slab + d, slabs), band), device_id_type=mesh_type
        )

    for other in others:
        pl.semaphore_signal(barrier, inc=1, device_id=(slab, other), device_id_type=mesh_type)
    pl.semaphore_wait(barrier, slabs - 1 + len(others))


def slab_sum(slabs, part_ref, landed, summed, sends, recvs):
    slab = lax.axis_index("slab")
    band = lax.axis_index("band")

    def scatter(d):
        peer = lax.rem(slab + d, slabs)
        return pltpu.make_async_remote_copy(
            src_ref=part_ref.at[peer],
            dst_ref=landed.at[d - 1],
            send_sem=sends.at[d - 1],
            recv_sem=recvs.at[d - 1],
            device_id=(peer, band),
            device_id_type=mesh_type,
        )

    @pl.loop(1, slabs)
    def _(d):
        scatter(d).start()

    summed[...] = part_ref[slab]

    @pl.loop(1, slabs)
    def _(d):
        scatter(d).wait()
        summed[...] += landed[d - 1]


def slab_spread(slabs, gathered, sends, recvs):
    slab = lax.axis_index("slab")
    band = lax.axis_index("band")

    def spread(d):
        return pltpu.make_async_remote_copy(
            src_ref=gathered.at[slab],
            dst_ref=gathered.at[slab],
            send_sem=sends.at[d - 1],
            recv_sem=recvs.at[d - 1],
            device_id=(lax.rem(slab + d, slabs), band),
            device_id_type=mesh_type,
        )

    @pl.loop(1, slabs)
    def _(d):
        spread(d).start()

    @pl.loop(1, slabs)
    def _(d):
        spread(d).wait()


def early_kernel(slabs, part_ref, out_ref, landed, summed, gathered, *sems):
    send_one, recv_one, send_two, recv_two = sems
    greet(slabs, ())
    slab_sum(slabs, part_ref, landed, summed, send_one, recv_one)
    gathered[lax.axis_index("slab")] = summed[...]
    slab_spread(slabs, gathered, send_two, recv_two)
    for block in range(out_ref.shape[0]):
        out_ref[block] = gathered[:, block].reshape(out_ref.shape[1:])


def late_kernel(
    slabs, part_ref, early_ref, overlap_ref, operator_ref,
    landed, summed, mirrored, gathered, crossed, send_one, recv_one, send_two, recv_two, send_three, recv_three,
):
    slab = lax.axis_index("slab")
    band = lax.axis_index("band")
    here_next = lax.rem(band + 1, groups)
    here_previous = lax.rem(band + groups - 1, groups)
    here_across = lax.rem(band + 2, groups)
    cols = overlap_ref.shape[1]

    greet(slabs, (here_next, here_previous, here_across))

    def exchange(source, target, place, other):
        return pltpu.make_async_remote_copy(
            src_ref=source,
            dst_ref=target,
            send_sem=send_two.at[place],
            recv_sem=recv_two.at[place],
            device_id=(slab, other),
            device_id_type=mesh_type,
        )

    crossing = exchange(early_ref.at[1], crossed, 0, here_across)
    crossing.start()
    slab_sum(slabs, part_ref, landed, summed, send_one, recv_one)
    mirror = exchange(summed.at[0], mirrored, 1, here_previous)
    mirror.start()
    mirror.wait()
    gathered[slab, 0] = summed[0]
    gathered[slab, 1] = mirrored[...]
    slab_spread(slabs, gathered, send_three, recv_three)
    crossing.wait()

    def place_rows(other, which):
        rows = pl.ds(pl.multiple_of(other * cols, cols), cols)
        for i, ref in enumerate((overlap_ref, operator_ref)):
            ref[rows, :] = which(i)

    gave = (band == across_round[0][0]) | (band == across_round[1][0])
    met = gathered[:, 0].reshape(2, cols, cols)
    back = gathered[:, 1].reshape(2, cols, cols)
    place_rows(band, lambda i: early_ref[0, i])
    place_rows(here_across, lambda i: jnp.where(gave, crossed[i].T, early_ref[1, i]))
    place_rows(here_previous, lambda i: met[i])
    place_rows(here_next, lambda i: back[i].T)


def pieces(parts, slabs):
    blocks, _, cols, _ = parts.shape
    return jnp.swapaxes(parts.reshape(blocks, slabs, 2 * cols // slabs, cols), 0, 1)


def early_reduce(parts, slabs):
    blocks, _, cols, _ = parts.shape
    rows = 2 * cols // slabs
    vmem = pl.BlockSpec(memory_space=pltpu.VMEM)
    return pl.pallas_call(
        functools.partial(early_kernel, slabs),
        out_shape=jax.ShapeDtypeStruct(parts.shape, jnp.float32),
        in_specs=[vmem],
        out_specs=vmem,
        scratch_shapes=[
            pltpu.VMEM((slabs - 1, blocks, rows, cols), jnp.float32),
            pltpu.VMEM((blocks, rows, cols), jnp.float32),
            pltpu.VMEM((slabs, blocks, rows, cols), jnp.float32),
        ]
        + [pltpu.SemaphoreType.DMA((slabs - 1,))] * 4,
        compiler_params=pltpu.CompilerParams(
            collective_id=0, has_side_effects=True, vmem_limit_bytes=32 * MIB
        ),
        name="early_reduce",
    )(pieces(parts, slabs))


def late_reduce(parts, early, slabs):
    blocks, _, cols, _ = parts.shape
    rows = 2 * cols // slabs
    vmem = pl.BlockSpec(memory_space=pltpu.VMEM)
    return pl.pallas_call(
        functools.partial(late_kernel, slabs),
        out_shape=(jax.ShapeDtypeStruct((groups * cols, cols), jnp.float32),) * 2,
        in_specs=[vmem, vmem],
        out_specs=(vmem, vmem),
        scratch_shapes=[
            pltpu.VMEM((slabs - 1, blocks, rows, cols), jnp.float32),
            pltpu.VMEM((blocks, rows, cols), jnp.float32),
            pltpu.VMEM((rows, cols), jnp.float32),
            pltpu.VMEM((slabs, 2, rows, cols), jnp.float32),
            pltpu.VMEM((2, cols, cols), jnp.float32),
            pltpu.SemaphoreType.DMA((slabs - 1,)),
            pltpu.SemaphoreType.DMA((slabs - 1,)),
            pltpu.SemaphoreType.DMA((2,)),
            pltpu.SemaphoreType.DMA((2,)),
            pltpu.SemaphoreType.DMA((slabs - 1,)),
            pltpu.SemaphoreType.DMA((slabs - 1,)),
        ],
        compiler_params=pltpu.CompilerParams(
            collective_id=1, has_side_effects=True, vmem_limit_bytes=32 * MIB
        ),
        name="late_reduce",
    )(pieces(parts, slabs), early)


def local(orbitals, potential, projector, strength, entry_slot, entry_block, entry_count):
    planes, height, cells, cols = orbitals.shape
    atom_slots, channels = strength.shape
    slots = 3 * atom_slots
    slabs = lax.axis_size("slab")
    up = [(i, (i + 1) % slabs) for i in range(slabs)]
    down = [(j, i) for i, j in up]

    met_across = lax.ppermute(orbitals, "band", across_round)
    met_next = lax.ppermute(orbitals, "band", next_round)
    before = lax.ppermute(orbitals, "slab", up)
    after = lax.ppermute(orbitals, "slab", down)

    weights, partial_value = project(
        entry_slot,
        entry_block,
        entry_count,
        projector,
        orbitals.reshape(planes * height, cells, cols),
        slots,
    )
    partial_value = partial_value.reshape(channels, 3, atom_slots, cols)
    from_left = lax.ppermute(partial_value[:, 2], "slab", up)
    from_right = lax.ppermute(partial_value[:, 0], "slab", down)
    coefficient = partial_value[:, 1] + from_left + from_right
    scaled = strength.T[:, :, None] * coefficient
    beside_all = jnp.stack(
        [lax.ppermute(scaled, "slab", up), scaled, lax.ppermute(scaled, "slab", down)], axis=1
    ).reshape(channels * slots, cols)

    applied = apply(orbitals, before, after, potential, beside_all, weights)

    volume = 1.0 / (slabs * planes * height * cells)
    early = early_reduce(gram((orbitals, met_across), orbitals, applied) * volume, slabs)
    late = gram((met_next,), orbitals, applied) * volume
    correlation, subspace = late_reduce(late, early, slabs)
    return applied, correlation, subspace


def solution(mesh):
    in_specs = (
        P("slab", None, None, "band"),
        P("slab", None, None),
        P("slab", None, None),
        P("slab", None),
        P("slab"),
        P("slab"),
        P("slab"),
    )
    out_specs = (P("slab", None, None, "band"), P(None, "band"), P(None, "band"))
    return jax.shard_map(local, mesh=mesh, in_specs=in_specs, out_specs=out_specs, check_vma=False)
```

```python
import functools

import jax
import jax.numpy as jnp
from jax import lax
from jax.experimental import pallas as pl
from jax.experimental.pallas import tpu as pltpu
from jax.sharding import PartitionSpec as P

centre_coef = -2.5
near_coef = 4.0 / 3.0
far_coef = -1.0 / 12.0
highest = lax.Precision.HIGHEST
MIB = 1 << 20

groups = 4
next_round = tuple((i, (i + 1) % groups) for i in range(groups))
across_round = ((0, 2), (3, 1))


def project_kernel(slots, slot_ref, block_ref, count_ref, projector_ref, x_ref, w_ref, part_ref):
    rows = x_ref.shape[0]
    channels = projector_ref.shape[1]

    @pl.loop(0, rows)
    def _(row):
        w_ref[row] = jnp.zeros(w_ref.shape[1:], jnp.float32)

    @pl.loop(0, count_ref[0])
    def _(entry):
        slot = slot_ref[entry]
        row = block_ref[entry]
        for channel in range(channels):
            place = pl.ds(channel * slots + slot, 1)
            w_ref[row, place, :] = (
                w_ref[row, place, :] + projector_ref[entry, pl.ds(channel, 1), :]
            )

    part_ref[...] = jnp.zeros_like(part_ref)

    @pl.loop(0, rows)
    def _(row):
        part_ref[...] += jnp.dot(
            w_ref[row], x_ref[row], precision=highest, preferred_element_type=jnp.float32
        )


def project(entry_slot, entry_block, entry_count, projector, grid_rows, slots):
    rows, cells, cols = grid_rows.shape
    channels = projector.shape[1]
    smem = pl.BlockSpec(memory_space=pltpu.SMEM)
    vmem = pl.BlockSpec(memory_space=pltpu.VMEM)
    return pl.pallas_call(
        functools.partial(project_kernel, slots),
        out_shape=(
            jax.ShapeDtypeStruct((rows, channels * slots, cells), jnp.float32),
            jax.ShapeDtypeStruct((channels * slots, cols), jnp.float32),
        ),
        in_specs=[smem, smem, smem, vmem, vmem],
        out_specs=(vmem, vmem),
        compiler_params=pltpu.CompilerParams(vmem_limit_bytes=48 * MIB),
        cost_estimate=pl.CostEstimate(
            flops=12 * rows * channels * slots * cells * cols,
            bytes_accessed=4 * rows * channels * slots * cells,
            transcendentals=0,
        ),
        name="project",
    )(entry_slot, entry_block, entry_count, projector, grid_rows)


def apply_kernel(x_ref, before_ref, after_ref, potential_ref, scaled_ref, w_ref, out_ref):
    planes, height, cells, cols = x_ref.shape
    y = pl.program_id(0)

    def plane(z, at):
        if z < 0:
            return before_ref[planes + z, at]
        if z >= planes:
            return after_ref[z - planes, at]
        return x_ref[z, at]

    for z in range(planes):
        centre = x_ref[z, y]
        near = plane(z - 1, y) + plane(z + 1, y)
        far = plane(z - 2, y) + plane(z + 2, y)
        near += x_ref[z, lax.rem(y + 1, height)] + x_ref[z, lax.rem(y + height - 1, height)]
        far += x_ref[z, lax.rem(y + 2, height)] + x_ref[z, lax.rem(y + height - 2, height)]
        near += pltpu.roll(centre, 1, 0) + pltpu.roll(centre, cells - 1, 0)
        far += pltpu.roll(centre, 2, 0) + pltpu.roll(centre, cells - 2, 0)
        level = jnp.broadcast_to(potential_ref[z, pl.ds(y, 1), :], (cols, cells)).T
        sphere = lax.dot_general(
            w_ref[z, 0],
            scaled_ref[...],
            (((0,), (0,)), ((), ())),
            precision=highest,
            preferred_element_type=jnp.float32,
        )
        out_ref[z, 0] = (
            (level - 1.5 * centre_coef) * centre
            - 0.5 * near_coef * near
            - 0.5 * far_coef * far
            + sphere
        )


def apply(orbitals, before, after, potential, scaled, weights):
    planes, height, cells, cols = orbitals.shape
    depth = weights.shape[1]
    vmem = pl.BlockSpec(memory_space=pltpu.VMEM)
    return pl.pallas_call(
        apply_kernel,
        grid=(height,),
        out_shape=jax.ShapeDtypeStruct(orbitals.shape, jnp.float32),
        in_specs=[vmem] * 5 + [pl.BlockSpec((planes, 1, depth, cells), lambda y: (0, y, 0, 0))],
        out_specs=pl.BlockSpec((planes, 1, cells, cols), lambda y: (0, y, 0, 0)),
        compiler_params=pltpu.CompilerParams(vmem_limit_bytes=48 * MIB),
        cost_estimate=pl.CostEstimate(
            flops=12 * planes * height * depth * cells * cols,
            bytes_accessed=4 * planes * height * depth * cells,
            transcendentals=0,
        ),
        name="apply",
    )(orbitals, before, after, potential, scaled, weights.reshape(planes, height, depth, cells))


def gram_kernel(count, scale, *refs):
    *left_refs, x_ref, applied_ref, out_ref, total = refs
    cols = x_ref.shape[1]
    bf16 = jnp.bfloat16

    def halves(values):
        high = values.astype(bf16)
        return high, (values - high.astype(jnp.float32)).astype(bf16)

    def times(left, right):
        return lax.dot_general(
            left, right, (((0,), (0,)), ((), ())), preferred_element_type=jnp.float32
        )

    @pl.when(pl.program_id(0) == 0)
    def _():
        total[...] = jnp.zeros_like(total)

    left_high, left_low = halves(jnp.concatenate([ref[...] for ref in left_refs], axis=1))
    right_high, right_low = halves(jnp.concatenate([x_ref[...], applied_ref[...]], axis=1))
    both = times(jnp.concatenate([left_high, left_low], axis=1), right_high)
    depth = count * cols
    total[...] += both[:depth] + both[depth:] + times(left_high, right_low)

    @pl.when(pl.program_id(0) == pl.num_programs(0) - 1)
    def _():
        for left in range(count):
            for right in range(2):
                out_ref[left, right] = scale * total[
                    left * cols : (left + 1) * cols, right * cols : (right + 1) * cols
                ]


def gram(lefts, orbitals, applied, scale):
    cols = orbitals.shape[-1]
    cells = orbitals.size // cols
    step = min(1024, cells)
    arrays = [x.reshape(cells, cols) for x in (*lefts, orbitals, applied)]
    count = len(lefts)
    return pl.pallas_call(
        functools.partial(gram_kernel, count, scale),
        grid=(cells // step,),
        out_shape=jax.ShapeDtypeStruct((count, 2, cols, cols), jnp.float32),
        in_specs=[pl.BlockSpec((step, cols), lambda i: (i, 0))] * len(arrays),
        out_specs=pl.BlockSpec((count, 2, cols, cols), lambda i: (0, 0, 0, 0)),
        scratch_shapes=[pltpu.VMEM((count * cols, 2 * cols), jnp.float32)],
        compiler_params=pltpu.CompilerParams(vmem_limit_bytes=60 * MIB),
        cost_estimate=pl.CostEstimate(
            flops=12 * count * cells * cols * cols,
            bytes_accessed=4 * (count + 2) * cells * cols,
            transcendentals=0,
        ),
        name="gram",
    )(*arrays)


mesh_type = pl.DeviceIdType.MESH


def greet(slabs, others):
    slab = lax.axis_index("slab")
    band = lax.axis_index("band")
    barrier = pltpu.get_barrier_semaphore()

    @pl.loop(1, slabs)
    def _(d):
        pl.semaphore_signal(
            barrier, inc=1, device_id=(lax.rem(slab + d, slabs), band), device_id_type=mesh_type
        )

    for other in others:
        pl.semaphore_signal(barrier, inc=1, device_id=(slab, other), device_id_type=mesh_type)
    pl.semaphore_wait(barrier, slabs - 1 + len(others))


def slab_sum(slabs, part_ref, landed, summed, sends, recvs):
    slab = lax.axis_index("slab")
    band = lax.axis_index("band")

    def scatter(d):
        peer = lax.rem(slab + d, slabs)
        return pltpu.make_async_remote_copy(
            src_ref=part_ref.at[peer],
            dst_ref=landed.at[d - 1],
            send_sem=sends.at[d - 1],
            recv_sem=recvs.at[d - 1],
            device_id=(peer, band),
            device_id_type=mesh_type,
        )

    @pl.loop(1, slabs)
    def _(d):
        scatter(d).start()

    summed[...] = part_ref[slab]

    @pl.loop(1, slabs)
    def _(d):
        scatter(d).wait()
        summed[...] += landed[d - 1]


def slab_spread(slabs, gathered, sends, recvs):
    slab = lax.axis_index("slab")
    band = lax.axis_index("band")

    def spread(d):
        return pltpu.make_async_remote_copy(
            src_ref=gathered.at[slab],
            dst_ref=gathered.at[slab],
            send_sem=sends.at[d - 1],
            recv_sem=recvs.at[d - 1],
            device_id=(lax.rem(slab + d, slabs), band),
            device_id_type=mesh_type,
        )

    @pl.loop(1, slabs)
    def _(d):
        spread(d).start()

    @pl.loop(1, slabs)
    def _(d):
        spread(d).wait()


def early_kernel(slabs, part_ref, out_ref, landed, summed, gathered, *sems):
    send_one, recv_one, send_two, recv_two = sems
    greet(slabs, ())
    slab_sum(slabs, part_ref, landed, summed, send_one, recv_one)
    gathered[lax.axis_index("slab")] = summed[...]
    slab_spread(slabs, gathered, send_two, recv_two)
    for block in range(out_ref.shape[0]):
        out_ref[block] = gathered[:, block].reshape(out_ref.shape[1:])


def late_kernel(
    slabs, part_ref, early_ref, overlap_ref, operator_ref,
    landed, summed, mirrored, gathered, crossed, send_one, recv_one, send_two, recv_two, send_three, recv_three,
):
    slab = lax.axis_index("slab")
    band = lax.axis_index("band")
    here_next = lax.rem(band + 1, groups)
    here_previous = lax.rem(band + groups - 1, groups)
    here_across = lax.rem(band + 2, groups)
    cols = overlap_ref.shape[1]

    greet(slabs, (here_next, here_previous, here_across))

    def exchange(source, target, place, other):
        return pltpu.make_async_remote_copy(
            src_ref=source,
            dst_ref=target,
            send_sem=send_two.at[place],
            recv_sem=recv_two.at[place],
            device_id=(slab, other),
            device_id_type=mesh_type,
        )

    crossing = exchange(early_ref.at[1], crossed, 0, here_across)
    crossing.start()
    slab_sum(slabs, part_ref, landed, summed, send_one, recv_one)
    mirror = exchange(summed.at[0], mirrored, 1, here_previous)
    mirror.start()
    mirror.wait()
    gathered[slab, 0] = summed[0]
    gathered[slab, 1] = mirrored[...]
    slab_spread(slabs, gathered, send_three, recv_three)
    crossing.wait()

    def place_rows(other, which):
        rows = pl.ds(pl.multiple_of(other * cols, cols), cols)
        for i, ref in enumerate((overlap_ref, operator_ref)):
            ref[rows, :] = which(i)

    gave = (band == across_round[0][0]) | (band == across_round[1][0])
    met = gathered[:, 0].reshape(2, cols, cols)
    back = gathered[:, 1].reshape(2, cols, cols)
    place_rows(band, lambda i: early_ref[0, i])
    place_rows(here_across, lambda i: jnp.where(gave, crossed[i].T, early_ref[1, i]))
    place_rows(here_previous, lambda i: met[i])
    place_rows(here_next, lambda i: back[i].T)


def pieces(parts, slabs):
    blocks, _, cols, _ = parts.shape
    return jnp.swapaxes(parts.reshape(blocks, slabs, 2 * cols // slabs, cols), 0, 1)


def early_reduce(parts, slabs):
    blocks, _, cols, _ = parts.shape
    rows = 2 * cols // slabs
    vmem = pl.BlockSpec(memory_space=pltpu.VMEM)
    return pl.pallas_call(
        functools.partial(early_kernel, slabs),
        out_shape=jax.ShapeDtypeStruct(parts.shape, jnp.float32),
        in_specs=[vmem],
        out_specs=vmem,
        scratch_shapes=[
            pltpu.VMEM((slabs - 1, blocks, rows, cols), jnp.float32),
            pltpu.VMEM((blocks, rows, cols), jnp.float32),
            pltpu.VMEM((slabs, blocks, rows, cols), jnp.float32),
        ]
        + [pltpu.SemaphoreType.DMA((slabs - 1,))] * 4,
        compiler_params=pltpu.CompilerParams(
            collective_id=0, has_side_effects=True, vmem_limit_bytes=32 * MIB
        ),
        name="early_reduce",
    )(pieces(parts, slabs))


def late_reduce(parts, early, slabs):
    blocks, _, cols, _ = parts.shape
    rows = 2 * cols // slabs
    vmem = pl.BlockSpec(memory_space=pltpu.VMEM)
    return pl.pallas_call(
        functools.partial(late_kernel, slabs),
        out_shape=(jax.ShapeDtypeStruct((groups * cols, cols), jnp.float32),) * 2,
        in_specs=[vmem, vmem],
        out_specs=(vmem, vmem),
        scratch_shapes=[
            pltpu.VMEM((slabs - 1, blocks, rows, cols), jnp.float32),
            pltpu.VMEM((blocks, rows, cols), jnp.float32),
            pltpu.VMEM((rows, cols), jnp.float32),
            pltpu.VMEM((slabs, 2, rows, cols), jnp.float32),
            pltpu.VMEM((2, cols, cols), jnp.float32),
            pltpu.SemaphoreType.DMA((slabs - 1,)),
            pltpu.SemaphoreType.DMA((slabs - 1,)),
            pltpu.SemaphoreType.DMA((2,)),
            pltpu.SemaphoreType.DMA((2,)),
            pltpu.SemaphoreType.DMA((slabs - 1,)),
            pltpu.SemaphoreType.DMA((slabs - 1,)),
        ],
        compiler_params=pltpu.CompilerParams(
            collective_id=1, has_side_effects=True, vmem_limit_bytes=32 * MIB
        ),
        name="late_reduce",
    )(pieces(parts, slabs), early)


def local(orbitals, potential, projector, strength, entry_slot, entry_block, entry_count):
    planes, height, cells, cols = orbitals.shape
    atom_slots, channels = strength.shape
    slots = 3 * atom_slots
    slabs = lax.axis_size("slab")
    up = [(i, (i + 1) % slabs) for i in range(slabs)]
    down = [(j, i) for i, j in up]

    met_across = lax.ppermute(orbitals, "band", across_round)
    met_next = lax.ppermute(orbitals, "band", next_round)
    before = lax.ppermute(orbitals, "slab", up)
    after = lax.ppermute(orbitals, "slab", down)

    weights, partial_value = project(
        entry_slot,
        entry_block,
        entry_count,
        projector,
        orbitals.reshape(planes * height, cells, cols),
        slots,
    )
    partial_value = partial_value.reshape(channels, 3, atom_slots, cols)
    from_left = lax.ppermute(partial_value[:, 2], "slab", up)
    from_right = lax.ppermute(partial_value[:, 0], "slab", down)
    coefficient = partial_value[:, 1] + from_left + from_right
    scaled = strength.T[:, :, None] * coefficient
    beside_all = jnp.stack(
        [lax.ppermute(scaled, "slab", up), scaled, lax.ppermute(scaled, "slab", down)], axis=1
    ).reshape(channels * slots, cols)

    applied = apply(orbitals, before, after, potential, beside_all, weights)

    volume = 1.0 / (slabs * planes * height * cells)
    early = early_reduce(gram((orbitals, met_across), orbitals, applied, volume), slabs)
    late = gram((met_next,), orbitals, applied, volume)
    correlation, subspace = late_reduce(late, early, slabs)
    return applied, correlation, subspace


def solution(mesh):
    in_specs = (
        P("slab", None, None, "band"),
        P("slab", None, None),
        P("slab", None, None),
        P("slab", None),
        P("slab"),
        P("slab"),
        P("slab"),
    )
    out_specs = (P("slab", None, None, "band"), P(None, "band"), P(None, "band"))
    return jax.shard_map(local, mesh=mesh, in_specs=in_specs, out_specs=out_specs, check_vma=False)
```
